128 devices in a mesh: dp: 8 (over z, core), tp: 16 (over y, x).
Axes of the slice: x: 4, y: 4, z: 4, core: 2. Of those that a mesh axis runs over, the one named last changes fastest.
Arguments:
- tokens: bfloat16 [8192, 3584], P('dp', 'tp'), may hold values from -6 to 6
- routes: int32 [8192, 8], P('dp'), may hold values from 0 to 127, all different within a row; in each aligned block of 1024 rows (0 to 1023, 1024 to 2047, ...) at most 66 rows name the same one
- route_weights: float32 [8192, 8], P('dp'), may hold values from 0.1 to 0.6
- expert_owner: int32 [128], replicated, may hold values from 0 to 127, each once
- expert_gate_up: bfloat16 [128, 3584, 2048], P(('dp', 'tp')), may hold values from -0.09375 to 0.09375
- expert_down: bfloat16 [128, 1024, 3584], P(('dp', 'tp')), may hold values from -0.1875 to 0.1875
- shared_gate_up: bfloat16 [3584, 2, 2048], P(None, None, 'tp'), may hold values from -0.09375 to 0.09375
- shared_down: bfloat16 [2048, 3584], P(None, 'tp'), may hold values from -0.125 to 0.125
Outputs:
- moe_output: bfloat16 [8192, 3584], P('dp', 'tp')
The draws below stay inside these ranges and needn't reach their ends.
Inputs may be any that keep to these rules, and one draw needn't show every extreme that they name: `routes`: in each aligned block of 1024 rows (the rows of one index of dp) no expert is named by more than 66 rows, a bound that some block reaches; each row names 8 different experts. A permutation: the device at position s of the mesh, dp-major, holds expert expert_owner[s].
All inputs are finite; a program needn't handle non-finite values.
Results may differ from the reference program's by a relative error of at most 0.0095.
Values may be sent and summed in bfloat16 or wider, within the bound.
No kernel may reach another device: no remote copies, remote signals or barrier semaphores. Data moves between devices by JAX's collectives and lax.ppermute only.
A program may use at most 192 MiB of HBM per device.

```python
import math
import jax
import jax.numpy as jnp
import numpy as np
from jax import lax

D = 3584
FFW = 1024
SFF = 2048
TOP = 8
TOK_DP = 1024
TOKENS = 8192
EXPERTS = 128
CAP = 66
N_DP = 8


def steps_of(own_key, shape, split, least, largest):
    def one(axis_at, parts):
        heights = jax.random.uniform(jax.random.fold_in(jax.random.fold_in(own_key, 6), axis_at), (parts,), jnp.float32, least / len(split), largest / len(split))
        return jnp.repeat(jnp.exp(heights), shape[axis_at] // parts).reshape((-1,) + (1,) * (len(shape) - axis_at - 1))

    loudness = one(*split[0])
    for cut in split[1:]:
        loudness = loudness * one(*cut)
    return loudness


def routed_block(key, own, number, rows, count, top, limit, skew):
    sequence = jax.random.permutation(key, count)
    heavy_load, usual = shares(count, rows * top, limit, skew, True), shares(count, rows * top, limit, skew, False)
    places = jnp.arange(count)

    def named(sizes, offset_by):
        used = int((sizes > 0).sum())
        fixed = max(1, used // 4)
        passed = fixed + (places - fixed + offset_by * (used - fixed)) % max(1, count - fixed)
        return jnp.zeros((count,), jnp.int32).at[sequence[jnp.where(places < fixed, places, passed)]].set(jnp.asarray(sizes, jnp.int32))

    sizes = jnp.where(number % 4 == 0, named(heavy_load, number // 4), named(usual, number - number // 4 - 1))
    mixed = jax.random.permutation(jax.random.fold_in(own, 3), count)
    donor, receiver = mixed[0:count // 2 * 2:2], mixed[1:count // 2 * 2:2]
    margin = jnp.minimum(sizes[donor] - 1, limit - sizes[receiver]) // 2
    margin = jnp.where((donor == sequence[0]) | (receiver == sequence[0]) | (sizes[receiver] == 0), 0, jnp.maximum(margin, 0))
    passed = jax.random.randint(jax.random.fold_in(own, 4), (count // 2,), 0, 1 << 20) % (margin + 1)
    sizes = sizes.at[donor].add(-passed).at[receiver].add(passed)
    labels = jnp.searchsorted(jnp.cumsum(sizes), jnp.arange(rows * top), side="right").astype(jnp.int32)
    grid = labels.reshape(top, rows).T
    grid = grid[jax.random.permutation(jax.random.fold_in(own, 1), rows)]
    offset_by = jax.random.randint(jax.random.fold_in(own, 2), (rows, 1), 0, top)
    return jnp.take_along_axis(grid, (jnp.arange(top)[None, :] + offset_by) % top, axis=1)


def shares(amount, total, most, slope, full):
    weights = [(1 << 20) // math.isqrt(rank ** slope) + 1 for rank in range(1, amount + 1)]
    largest = most if full else min(most, max(-(-total // amount), total * weights[0] // sum(weights)))
    least = 1 if total - largest >= amount - 1 else 0
    holding, surplus = [largest] + [least] * (amount - 1), total - largest - least * (amount - 1)
    while surplus > 0:
        free = [i for i in range(1, amount) if holding[i] < largest] or [i for i in range(1, amount) if holding[i] < most]
        pool, left = sum([weights[i] for i in free]), surplus
        for i in free:
            more = min(most - holding[i], max(1, left * weights[i] // pool), surplus)
            holding[i] = holding[i] + more
            surplus = surplus - more
    return np.array(holding)


def scatter_about(own_key, shape, deviation, bound, shards=(), kind=jnp.bfloat16):
    loudness = steps_of(own_key, shape, shards, -0.22, 0.18) if shards else 1.0
    array = jax.random.normal(own_key, shape, jnp.float32) * deviation * loudness
    return jnp.minimum(jnp.maximum(array, -bound), bound).astype(kind)


def setup_inputs(seed: int = 0) -> dict:
    key_of = jax.random.split(jax.random.key(seed), 9)
    tokens = scatter_about(key_of[0], (TOKENS, D), 1.0, 6.0, ((0, 8), (1, 16)))
    routes_keys = jax.random.split(jax.random.fold_in(key_of[1], 1), TOKENS // TOK_DP)
    routes_turns = jax.random.permutation(jax.random.fold_in(key_of[1], 3), TOKENS // TOK_DP)
    routes = jax.vmap(lambda own, number: routed_block(jax.random.fold_in(key_of[1], 2), own, number, TOK_DP, EXPERTS, TOP, CAP, 2))(routes_keys, routes_turns).reshape((TOKENS, TOP))
    route_weights = jnp.clip(0.1 + 0.5 * jax.random.uniform(key_of[2], (TOKENS, TOP), jnp.float32) ** steps_of(key_of[2], (TOKENS, TOP), ((0, 8),), -0.2, 0.2), 0.1, 0.6)
    expert_owner = jax.random.permutation(key_of[3], EXPERTS).astype(jnp.int32)
    expert_gate_up = scatter_about(key_of[4], (EXPERTS, D, 2 * FFW), D ** -0.5, 0.09375, ((0, 128),))
    expert_down = scatter_about(key_of[5], (EXPERTS, FFW, D), FFW ** -0.5, 0.1875, ((0, 128),))
    shared_gate_up = scatter_about(key_of[6], (D, 2, SFF), D ** -0.5, 0.09375, ((2, 16),))
    shared_down = scatter_about(key_of[7], (SFF, D), SFF ** -0.5, 0.125, ((1, 16),))
    return {"tokens": tokens, "routes": routes, "route_weights": route_weights, "expert_owner": expert_owner, "expert_gate_up": expert_gate_up, "expert_down": expert_down, "shared_gate_up": shared_gate_up, "shared_down": shared_down}


def reference(tokens, routes, route_weights, expert_owner, expert_gate_up, expert_down, shared_gate_up, shared_down):
    model_width = tokens.shape[1]
    shared_proj = jnp.dot(tokens, shared_gate_up.reshape(model_width, 2 * SFF), preferred_element_type=jnp.float32)
    shared_act = (jax.nn.silu(shared_proj[:, :SFF]) * shared_proj[:, SFF:]).astype(jnp.bfloat16)
    shared_out = jnp.dot(shared_act, shared_down, preferred_element_type=jnp.float32)
    row_limit = N_DP * CAP

    def one_slot(slot_index, running):
        expert = expert_owner[slot_index]
        matched = routes == expert
        picked = jnp.any(matched, axis=1)
        weight = jnp.sum(jnp.where(matched, route_weights, jnp.float32(0.0)), axis=1)
        rows_index = jnp.nonzero(picked, size=row_limit, fill_value=0)[0].astype(jnp.int32)
        is_live = jnp.arange(row_limit, dtype=jnp.int32) < jnp.sum(picked.astype(jnp.int32))
        chosen_rows = tokens[rows_index]
        projected = jnp.dot(chosen_rows, expert_gate_up[slot_index], preferred_element_type=jnp.float32)
        activated = (jax.nn.silu(projected[:, :FFW]) * projected[:, FFW:]).astype(jnp.bfloat16)
        result = jnp.dot(activated, expert_down[slot_index], preferred_element_type=jnp.float32).astype(jnp.bfloat16)
        factor = jnp.where(is_live, weight[rows_index], jnp.float32(0.0))
        scaled = result.astype(jnp.float32) * factor[:, None]
        return running.at[rows_index].add(scaled)

    routed = lax.fori_loop(0, EXPERTS, one_slot, jnp.zeros((TOKENS, D), jnp.float32))
    return (shared_out + routed).astype(jnp.bfloat16)
```

```python
import functools

import jax
import jax.numpy as jnp
from jax import lax
from jax.experimental import pallas as pl
from jax.experimental.pallas import tpu as pltpu
from jax.sharding import PartitionSpec as P

F32 = jnp.float32
BF16 = jnp.bfloat16
SIDE = 4
ROW = 72
PACK = 120
VMEM = 40 * 1024 * 1024


def params(semantics=None, vmem=VMEM):
    return pltpu.CompilerParams(vmem_limit_bytes=vmem, dimension_semantics=semantics)


def whole(space=pltpu.VMEM):
    return pl.BlockSpec(memory_space=space)


def dot(a, b, dims):
    return lax.dot_general(a, b, (dims, ((), ())), preferred_element_type=F32)


def pack(low, high):
    lane = lax.broadcasted_iota(jnp.int32, (48, 128), 1)
    line = lax.broadcasted_iota(jnp.int32, (8, 128), 0)
    tail = high[48:64]
    moved = jnp.concatenate([pltpu.roll(tail, 96 - 32 * q, 1) for q in range(3)], axis=0)
    second = jnp.where(lane < 96, high[:48], moved)
    extra = jnp.where(line < 2, low[64:72], pltpu.roll(high[64:72], 2, 0))
    return jnp.concatenate([low[:64], second, extra], axis=0).astype(BF16)


def unpack_tail(second):
    lane = lax.broadcasted_iota(jnp.int32, (16, 128), 1)
    tail = jnp.zeros((16, 128), F32)
    for q in range(3):
        moved = pltpu.roll(second[16 * q : 16 * q + 16], 32 + 32 * q, 1)
        tail = jnp.where((lane >= 32 * q) & (lane < 32 * q + 32), moved, tail)
    return tail


def unpack(block):
    block = block.astype(F32)
    line = lax.broadcasted_iota(jnp.int32, (8, 128), 0)
    second, extra = block[64:112], block[112:120]
    low = jnp.concatenate([block[:64], jnp.where(line < 2, extra, 0.0)], axis=0)
    last = jnp.where(line < 2, pltpu.roll(extra, 6, 0), 0.0)
    high = jnp.concatenate([second, unpack_tail(second), last], axis=0)
    return jnp.concatenate([low, high[:, :96]], axis=1)


def dispatch_kernel(per_step, routes_ref, weights_ref, owner_ref, tokens_ref, rank_ref, weight_ref, out_ref):
    experts, tokens = rank_ref.shape
    feats = tokens_ref.shape[0]
    step = pl.program_id(0)

    @pl.when(step == 0)
    def _():
        owner = jnp.broadcast_to(owner_ref[...], (experts, experts)).astype(F32).T[:, :1]
        routes = routes_ref[...].astype(F32)
        hit = jnp.zeros((experts, tokens), F32)
        weight = jnp.zeros((experts, tokens), F32)
        for k in range(routes_ref.shape[0]):
            same = owner == routes[k : k + 1, :]
            hit = jnp.where(same, 1.0, hit)
            weight = jnp.where(same, weights_ref[k : k + 1, :], weight)
        weight_ref[...] = weight
        earlier = lax.broadcasted_iota(jnp.int32, (tokens, tokens), 0)
        later = lax.broadcasted_iota(jnp.int32, (tokens, tokens), 1)
        before = jnp.where(earlier < later, 1.0, 0.0).astype(BF16)
        rank = dot(hit.astype(BF16), before, ((1,), (0,)))
        rank_ref[...] = jnp.where(hit > 0.0, rank, -1.0)

    place = lax.broadcasted_iota(jnp.int32, (ROW, tokens), 0).astype(F32)
    rank = rank_ref[pl.ds(pl.multiple_of(step * per_step, per_step), per_step), :]
    pick = [jnp.where(place == rank[e : e + 1, :], 1.0, 0.0) for e in range(per_step)]
    pick = jnp.concatenate(pick, axis=0).astype(BF16)
    feat = jnp.concatenate([tokens_ref[...], jnp.zeros((256 - feats, tokens), BF16)], axis=0)
    res = dot(pick, feat, ((1,), (1,)))
    for e in range(per_step):
        rows = res[e * ROW : (e + 1) * ROW]
        out_ref[e] = pack(rows[:, :128], rows[:, 128:])


def dispatch(routes, weights, owner, tokens, per_step=16):
    experts, count = owner.shape[1], routes.shape[1]
    fixed = lambda a: pl.BlockSpec(a.shape, lambda i: (0, 0))
    table = jax.ShapeDtypeStruct((experts, count), F32)
    return pl.pallas_call(
        functools.partial(dispatch_kernel, per_step),
        out_shape=(table, table, jax.ShapeDtypeStruct((experts, PACK, 128), BF16)),
        grid=(experts // per_step,),
        in_specs=[fixed(routes), fixed(weights), fixed(owner), fixed(tokens)],
        out_specs=(
            fixed(table),
            fixed(table),
            pl.BlockSpec((per_step, PACK, 128), lambda i: (i, 0, 0)),
        ),
        compiler_params=params(("arbitrary",), 60 * 1024 * 1024),
        cost_estimate=pl.CostEstimate(
            flops=2 * experts * ROW * 256 * count, bytes_accessed=6 * 10**6, transcendentals=0
        ),
    )(routes, weights, owner, tokens)


def expert_kernel(tile, got_in, up_in, down_in, out_ref, got, up_w, down_w, x, act, held, sems):
    groups, n_tensor = out_ref.shape[:2]
    share = n_tensor // SIDE
    hidden = act.shape[1]
    wide = x.shape[1] // SIDE
    feats = wide // share
    tiles = hidden // tile

    def got_copy(k):
        return pltpu.make_async_copy(
            got_in.at[:, pl.ds(k * share, share)], got.at[k], sems.at[k]
        )

    def up_copy(n):
        cols = pl.ds(n * tile, tile)
        return pltpu.make_async_copy(up_in.at[:, cols], up_w.at[:, cols], sems.at[SIDE + n])

    def down_copy(y):
        cols = pl.ds(y * wide, wide)
        at = SIDE + 2 * tiles + y
        return pltpu.make_async_copy(down_in.at[:, cols], down_w.at[:, cols], sems.at[at])

    def out_copy(y):
        at = 2 * SIDE + 2 * tiles + y
        return pltpu.make_async_copy(
            held.at[y], out_ref.at[:, pl.ds(y * share, share)], sems.at[at]
        )

    for k in range(SIDE):
        got_copy(k).start()
    for n in range(tiles):
        up_copy(n).start()
        up_copy(tiles + n).start()
    for y in range(SIDE):
        down_copy(y).start()

    for k in range(SIDE):
        got_copy(k).wait()
        for d in range(0, groups, 2):
            rows = []
            for i in (d, d + 1):
                parts = [unpack(got[k, i, t]) for t in range(share)]
                rows.append(jnp.concatenate(parts, axis=1))
            x[d * ROW : (d + 2) * ROW, k * wide : (k + 1) * wide] = jnp.concatenate(
                rows, axis=0
            ).astype(BF16)

    for n in range(tiles):
        up_copy(n).wait()
        up_copy(tiles + n).wait()
        low = slice(n * tile, (n + 1) * tile)
        high = slice(hidden + n * tile, hidden + (n + 1) * tile)
        gate = dot(x[...], up_w[:, low], ((1,), (0,)))
        up = dot(x[...], up_w[:, high], ((1,), (0,)))
        act[:, low] = (gate / (1.0 + jnp.exp(-gate)) * up).astype(BF16)

    for y in range(SIDE):
        down_copy(y).wait()
        res = dot(act[...], down_w[:, y * wide : (y + 1) * wide], ((1,), (0,)))
        for t in range(share):
            low = res[:, t * feats : t * feats + 128]
            high = res[:, t * feats + 128 : (t + 1) * feats]
            blank = jnp.zeros((res.shape[0], 256 - feats), F32)
            high = jnp.concatenate([high, blank], axis=1)
            for d in range(groups):
                block = slice(d * ROW, (d + 1) * ROW)
                held[y, d, t] = pack(low[block], high[block])
        out_copy(y).start()
    for y in range(SIDE):
        out_copy(y).wait()


def expert(got, up_weights, down_weights, tile=256):
    groups, n_tensor = got.shape[:2]
    rows = groups * ROW
    width, both = up_weights.shape
    hidden = both // 2
    blocks = pltpu.VMEM((SIDE, groups, n_tensor // SIDE, PACK, 128), BF16)
    return pl.pallas_call(
        functools.partial(expert_kernel, tile),
        out_shape=jax.ShapeDtypeStruct(got.shape, BF16),
        in_specs=[whole(pl.ANY)] * 3,
        out_specs=whole(pl.ANY),
        scratch_shapes=[
            blocks,
            pltpu.VMEM((width, both), BF16),
            pltpu.VMEM((hidden, width), BF16),
            pltpu.VMEM((rows, width), BF16),
            pltpu.VMEM((rows, hidden), BF16),
            blocks,
            pltpu.SemaphoreType.DMA((3 * SIDE + both // tile,)),
        ],
        compiler_params=params(vmem=60 * 1024 * 1024),
        cost_estimate=pl.CostEstimate(
            flops=6 * rows * width * hidden, bytes_accessed=6 * width * hidden, transcendentals=0
        ),
    )(got, up_weights, down_weights)


def spread_kernel(rank_ref, weight_ref, main_ref, late_ref):
    experts, tokens = rank_ref.shape
    place = lax.broadcasted_iota(jnp.int32, (64, tokens), 0).astype(F32)
    line = lax.broadcasted_iota(jnp.int32, (8, tokens), 0)
    late = jnp.where(line < 4, jnp.where(line % 2 == 0, 64.0, 65.0), -2.0)
    extra = []
    for e in range(0, experts, 2):
        pair = []
        for i in (e, e + 1):
            rank = rank_ref[i : i + 1, :]
            weight = weight_ref[i : i + 1, :]
            pair.append(jnp.where(place == rank, weight, 0.0))
            extra.append(jnp.where(late == rank, weight, 0.0))
        main_ref[:, e * 64 : (e + 2) * 64] = jnp.concatenate(pair, axis=0).astype(BF16).T
    late_ref[...] = jnp.concatenate(extra, axis=0).astype(BF16).T


def spread(rank, weight, per_step=16):
    experts, tokens = rank.shape
    lines = pl.BlockSpec((per_step, tokens), lambda i: (i, 0))
    block = lambda rows: pl.BlockSpec((tokens, per_step * rows), lambda i: (0, i))
    return pl.pallas_call(
        spread_kernel,
        out_shape=(
            jax.ShapeDtypeStruct((tokens, experts * 64), BF16),
            jax.ShapeDtypeStruct((tokens, experts * 8), BF16),
        ),
        grid=(experts // per_step,),
        in_specs=[lines, lines],
        out_specs=(block(64), block(8)),
        compiler_params=params(("arbitrary",), 60 * 1024 * 1024),
        cost_estimate=pl.CostEstimate(
            flops=2 * experts * 64 * tokens, bytes_accessed=20 * 10**6, transcendentals=0
        ),
    )(rank, weight)


def combine_kernel(steps, back_ref, main_ref, late_ref, shared_ref, out_ref, total):
    step = pl.program_id(0)
    line = lax.broadcasted_iota(jnp.int32, (8, 128), 0)
    left, right, extra_l, extra_r = [], [], [], []
    for e in range(back_ref.shape[0]):
        left.append(back_ref[e, 0:64, :])
        second = back_ref[e, 64:112, :]
        tail = unpack_tail(second.astype(F32)).astype(BF16)
        right.append(jnp.concatenate([second, tail], axis=0))
        extra = back_ref[e, 112:120, :].astype(F32)
        extra_l.append(jnp.where(line < 2, extra, 0.0))
        extra_r.append(jnp.where((line >= 2) & (line < 4), extra, 0.0))
    rows = jnp.concatenate([jnp.concatenate(left, axis=0), jnp.concatenate(right, axis=0)], axis=1)
    late_rows = jnp.concatenate(
        [jnp.concatenate(extra_l, axis=0), jnp.concatenate(extra_r, axis=0)], axis=1
    ).astype(BF16)
    part = dot(main_ref[...], rows, ((1,), (0,))) + dot(late_ref[...], late_rows, ((1,), (0,)))

    @pl.when(step == 0)
    def _():
        total[...] = part

    @pl.when((step > 0) & (step < steps - 1))
    def _():
        total[...] += part

    @pl.when(step == steps - 1)
    def _():
        feats = out_ref.shape[0]
        out_ref[...] = ((total[...] + part).T[:feats] + shared_ref[...]).astype(BF16)


def combine(back, main, late, shared, per_step=32):
    experts = back.shape[0]
    tokens = main.shape[0]
    feats = shared.shape[0]
    steps = experts // per_step
    return pl.pallas_call(
        functools.partial(combine_kernel, steps),
        out_shape=jax.ShapeDtypeStruct((feats, tokens), BF16),
        grid=(steps,),
        in_specs=[
            pl.BlockSpec((per_step, PACK, 128), lambda i: (i, 0, 0)),
            pl.BlockSpec((tokens, per_step * 64), lambda i: (0, i)),
            pl.BlockSpec((tokens, per_step * 8), lambda i: (0, i)),
            pl.BlockSpec((feats, tokens), lambda i: (0, 0)),
        ],
        out_specs=pl.BlockSpec((feats, tokens), lambda i: (0, 0)),
        scratch_shapes=[pltpu.VMEM((tokens, 256), F32)],
        compiler_params=params(("arbitrary",), 56 * 1024 * 1024),
        cost_estimate=pl.CostEstimate(
            flops=2 * experts * 72 * 256 * tokens, bytes_accessed=24 * 10**6, transcendentals=0
        ),
    )(back, main, late, shared)


def on_device(
    tokens,
    routes,
    route_weights,
    expert_owner,
    expert_gate_up,
    expert_down,
    shared_gate_up,
    shared_down,
):
    groups = lax.axis_size("dp")
    n_tensor = lax.axis_size("tp")
    experts = groups * n_tensor
    features = tokens.T
    features_all = lax.all_gather(features, "tp", axis=0, tiled=True)
    rank, weight, blocks = dispatch(
        routes.T, route_weights.T, expert_owner.reshape(1, -1), features
    )

    def exchange(blocks):
        return lax.all_to_all(blocks, ("dp", "tp"), split_axis=0, concat_axis=0, tiled=True)

    got = exchange(blocks).reshape(groups, n_tensor, PACK, 128)
    packed = expert(got, expert_gate_up[0], expert_down[0])

    shared_gate_up, _ = lax.optimization_barrier((shared_gate_up, packed))
    shared_w = shared_gate_up.reshape(features_all.shape[0], -1)
    proj = dot(shared_w, features_all, ((0,), (0,)))
    units = proj.shape[0] // 2
    shared_act = (jax.nn.silu(proj[:units]) * proj[units:]).astype(BF16)
    shared_all = lax.all_gather(shared_act, "tp", axis=0, tiled=True)

    main, late = spread(rank, weight)
    back = exchange(packed.reshape(experts, PACK, 128))
    shared_out = dot(shared_down.T, shared_all, ((1,), (0,)))
    return combine(back, main, late, shared_out).T


def solution(mesh):
    return jax.shard_map(
        on_device,
        mesh=mesh,
        in_specs=(
            P("dp", "tp"),
            P("dp", None),
            P("dp", None),
            P(),
            P(("dp", "tp"), None, None),
            P(("dp", "tp"), None, None),
            P(None, None, "tp"),
            P(None, "tp"),
        ),
        out_specs=P("dp", "tp"),
        check_vma=False,
    )
```

```python
import functools

import jax
import jax.numpy as jnp
from jax import lax
from jax.experimental import pallas as pl
from jax.experimental.pallas import tpu as pltpu
from jax.sharding import PartitionSpec as P

F32 = jnp.float32
BF16 = jnp.bfloat16
SIDE = 4
ROW = 72
PACK = 120
VMEM = 40 * 1024 * 1024


def params(semantics=None, vmem=VMEM):
    return pltpu.CompilerParams(vmem_limit_bytes=vmem, dimension_semantics=semantics)


def whole(space=pltpu.VMEM):
    return pl.BlockSpec(memory_space=space)


def dot(a, b, dims):
    return lax.dot_general(a, b, (dims, ((), ())), preferred_element_type=F32)


def pack(low, high):
    lane = lax.broadcasted_iota(jnp.int32, (48, 128), 1)
    line = lax.broadcasted_iota(jnp.int32, (8, 128), 0)
    tail = high[48:64]
    moved = jnp.concatenate([pltpu.roll(tail, 96 - 32 * q, 1) for q in range(3)], axis=0)
    second = jnp.where(lane < 96, high[:48], moved)
    extra = jnp.where(line < 2, low[64:72], pltpu.roll(high[64:72], 2, 0))
    return jnp.concatenate([low[:64], second, extra], axis=0).astype(BF16)


def unpack_tail(second):
    lane = lax.broadcasted_iota(jnp.int32, (16, 128), 1)
    tail = jnp.zeros((16, 128), F32)
    for q in range(3):
        moved = pltpu.roll(second[16 * q : 16 * q + 16], 32 + 32 * q, 1)
        tail = jnp.where((lane >= 32 * q) & (lane < 32 * q + 32), moved, tail)
    return tail


def unpack(block):
    block = block.astype(F32)
    line = lax.broadcasted_iota(jnp.int32, (8, 128), 0)
    second, extra = block[64:112], block[112:120]
    low = jnp.concatenate([block[:64], jnp.where(line < 2, extra, 0.0)], axis=0)
    last = jnp.where(line < 2, pltpu.roll(extra, 6, 0), 0.0)
    high = jnp.concatenate([second, unpack_tail(second), last], axis=0)
    return jnp.concatenate([low, high[:, :96]], axis=1)


def dispatch_kernel(per_step, routes_ref, weights_ref, owner_ref, tokens_ref, rank_ref, weight_ref, out_ref):
    experts, tokens = rank_ref.shape
    feats = tokens_ref.shape[0]
    step = pl.program_id(0)

    @pl.when(step == 0)
    def _():
        owner = jnp.broadcast_to(owner_ref[...], (experts, experts)).astype(F32).T[:, :1]
        routes = routes_ref[...].astype(F32)
        hit = jnp.zeros((experts, tokens), F32)
        weight = jnp.zeros((experts, tokens), F32)
        for k in range(routes_ref.shape[0]):
            same = owner == routes[k : k + 1, :]
            hit = jnp.where(same, 1.0, hit)
            weight = jnp.where(same, weights_ref[k : k + 1, :], weight)
        weight_ref[...] = weight
        earlier = lax.broadcasted_iota(jnp.int32, (tokens, tokens), 0)
        later = lax.broadcasted_iota(jnp.int32, (tokens, tokens), 1)
        before = jnp.where(earlier < later, 1.0, 0.0).astype(BF16)
        rank = dot(hit.astype(BF16), before, ((1,), (0,)))
        rank_ref[...] = jnp.where(hit > 0.0, rank, -1.0)

    place = lax.broadcasted_iota(jnp.int32, (ROW, tokens), 0).astype(F32)
    rank = rank_ref[pl.ds(pl.multiple_of(step * per_step, per_step), per_step), :]
    pick = [jnp.where(place == rank[e : e + 1, :], 1.0, 0.0) for e in range(per_step)]
    pick = jnp.concatenate(pick, axis=0).astype(BF16)
    feat = jnp.concatenate([tokens_ref[...], jnp.zeros((256 - feats, tokens), BF16)], axis=0)
    res = dot(pick, feat, ((1,), (1,)))
    for e in range(per_step):
        rows = res[e * ROW : (e + 1) * ROW]
        out_ref[e] = pack(rows[:, :128], rows[:, 128:])


def dispatch(routes, weights, owner, tokens, per_step=16):
    experts, count = owner.shape[1], routes.shape[1]
    fixed = lambda a: pl.BlockSpec(a.shape, lambda i: (0, 0))
    table = jax.ShapeDtypeStruct((experts, count), F32)
    return pl.pallas_call(
        functools.partial(dispatch_kernel, per_step),
        out_shape=(table, table, jax.ShapeDtypeStruct((experts, PACK, 128), BF16)),
        grid=(experts // per_step,),
        in_specs=[fixed(routes), fixed(weights), fixed(owner), fixed(tokens)],
        out_specs=(
            fixed(table),
            fixed(table),
            pl.BlockSpec((per_step, PACK, 128), lambda i: (i, 0, 0)),
        ),
        compiler_params=params(("arbitrary",), 60 * 1024 * 1024),
        cost_estimate=pl.CostEstimate(
            flops=2 * experts * ROW * 256 * count, bytes_accessed=6 * 10**6, transcendentals=0
        ),
    )(routes, weights, owner, tokens)


def expert_kernel(tile, got_in, up_in, down_in, out_ref, got, up_w, down_w, x, act, held, sems):
    groups, n_tensor = out_ref.shape[:2]
    share = n_tensor // SIDE
    hidden = act.shape[1]
    wide = x.shape[1] // SIDE
    feats = wide // share
    tiles = hidden // tile

    def got_copy(k):
        return pltpu.make_async_copy(
            got_in.at[:, pl.ds(k * share, share)], got.at[k], sems.at[k]
        )

    def up_copy(n):
        cols = pl.ds(n * tile, tile)
        return pltpu.make_async_copy(up_in.at[:, cols], up_w.at[:, cols], sems.at[SIDE + n])

    def down_copy(y):
        cols = pl.ds(y * wide, wide)
        at = SIDE + 2 * tiles + y
        return pltpu.make_async_copy(down_in.at[:, cols], down_w.at[:, cols], sems.at[at])

    def out_copy(y):
        at = 2 * SIDE + 2 * tiles + y
        return pltpu.make_async_copy(
            held.at[y], out_ref.at[:, pl.ds(y * share, share)], sems.at[at]
        )

    for k in range(SIDE):
        got_copy(k).start()
    for n in range(tiles):
        up_copy(n).start()
        up_copy(tiles + n).start()
    for y in range(SIDE):
        down_copy(y).start()

    for k in range(SIDE):
        got_copy(k).wait()
        for d in range(0, groups, 2):
            rows = []
            for i in (d, d + 1):
                parts = [unpack(got[k, i, t]) for t in range(share)]
                rows.append(jnp.concatenate(parts, axis=1))
            x[d * ROW : (d + 2) * ROW, k * wide : (k + 1) * wide] = jnp.concatenate(
                rows, axis=0
            ).astype(BF16)

    for n in range(tiles):
        up_copy(n).wait()
        up_copy(tiles + n).wait()
        low = slice(n * tile, (n + 1) * tile)
        high = slice(hidden + n * tile, hidden + (n + 1) * tile)
        gate = dot(x[...], up_w[:, low], ((1,), (0,)))
        up = dot(x[...], up_w[:, high], ((1,), (0,)))
        act[:, low] = (gate / (1.0 + jnp.exp(-gate)) * up).astype(BF16)

    for y in range(SIDE):
        down_copy(y).wait()
        res = dot(act[...], down_w[:, y * wide : (y + 1) * wide], ((1,), (0,)))
        for t in range(share):
            low = res[:, t * feats : t * feats + 128]
            high = res[:, t * feats + 128 : (t + 1) * feats]
            blank = jnp.zeros((res.shape[0], 256 - feats), F32)
            high = jnp.concatenate([high, blank], axis=1)
            for d in range(groups):
                block = slice(d * ROW, (d + 1) * ROW)
                held[y, d, t] = pack(low[block], high[block])
        out_copy(y).start()
    for y in range(SIDE):
        out_copy(y).wait()


def expert(got, up_weights, down_weights, tile=256):
    groups, n_tensor = got.shape[:2]
    rows = groups * ROW
    width, both = up_weights.shape
    hidden = both // 2
    blocks = pltpu.VMEM((SIDE, groups, n_tensor // SIDE, PACK, 128), BF16)
    return pl.pallas_call(
        functools.partial(expert_kernel, tile),
        out_shape=jax.ShapeDtypeStruct(got.shape, BF16),
        in_specs=[whole(pl.ANY)] * 3,
        out_specs=whole(pl.ANY),
        scratch_shapes=[
            blocks,
            pltpu.VMEM((width, both), BF16),
            pltpu.VMEM((hidden, width), BF16),
            pltpu.VMEM((rows, width), BF16),
            pltpu.VMEM((rows, hidden), BF16),
            blocks,
            pltpu.SemaphoreType.DMA((3 * SIDE + both // tile,)),
        ],
        compiler_params=params(vmem=60 * 1024 * 1024),
        cost_estimate=pl.CostEstimate(
            flops=6 * rows * width * hidden, bytes_accessed=6 * width * hidden, transcendentals=0
        ),
    )(got, up_weights, down_weights)


def spread_kernel(rank_ref, weight_ref, main_ref, late_ref):
    experts, tokens = rank_ref.shape
    place = lax.broadcasted_iota(jnp.int32, (64, tokens), 0).astype(F32)
    line = lax.broadcasted_iota(jnp.int32, (8, tokens), 0)
    late = jnp.where(line < 4, jnp.where(line % 2 == 0, 64.0, 65.0), -2.0)
    extra = []
    for e in range(0, experts, 2):
        pair = []
        for i in (e, e + 1):
            rank = rank_ref[i : i + 1, :]
            weight = weight_ref[i : i + 1, :]
            pair.append(jnp.where(place == rank, weight, 0.0))
            extra.append(jnp.where(late == rank, weight, 0.0))
        main_ref[:, e * 64 : (e + 2) * 64] = jnp.concatenate(pair, axis=0).astype(BF16).T
    late_ref[...] = jnp.concatenate(extra, axis=0).astype(BF16).T


def spread(rank, weight, per_step=16):
    experts, tokens = rank.shape
    lines = pl.BlockSpec((per_step, tokens), lambda i: (i, 0))
    block = lambda rows: pl.BlockSpec((tokens, per_step * rows), lambda i: (0, i))
    return pl.pallas_call(
        spread_kernel,
        out_shape=(
            jax.ShapeDtypeStruct((tokens, experts * 64), BF16),
            jax.ShapeDtypeStruct((tokens, experts * 8), BF16),
        ),
        grid=(experts // per_step,),
        in_specs=[lines, lines],
        out_specs=(block(64), block(8)),
        compiler_params=params(("arbitrary",), 60 * 1024 * 1024),
        cost_estimate=pl.CostEstimate(
            flops=2 * experts * 64 * tokens, bytes_accessed=20 * 10**6, transcendentals=0
        ),
    )(rank, weight)


def combine_kernel(last, back_ref, main_ref, late_ref, *refs):
    step = pl.program_id(0)
    total = refs[-1]
    line = lax.broadcasted_iota(jnp.int32, (8, 128), 0)
    left, right, extra_l, extra_r = [], [], [], []
    for e in range(back_ref.shape[0]):
        left.append(back_ref[e, 0:64, :])
        second = back_ref[e, 64:112, :]
        tail = unpack_tail(second.astype(F32)).astype(BF16)
        right.append(jnp.concatenate([second, tail], axis=0))
        extra = back_ref[e, 112:120, :].astype(F32)
        extra_l.append(jnp.where(line < 2, extra, 0.0))
        extra_r.append(jnp.where((line >= 2) & (line < 4), extra, 0.0))
    rows = jnp.concatenate([jnp.concatenate(left, axis=0), jnp.concatenate(right, axis=0)], axis=1)
    late_rows = jnp.concatenate(
        [jnp.concatenate(extra_l, axis=0), jnp.concatenate(extra_r, axis=0)], axis=1
    ).astype(BF16)
    part = dot(main_ref[...], rows, ((1,), (0,))) + dot(late_ref[...], late_rows, ((1,), (0,)))

    @pl.when(step == 0)
    def _():
        total[...] = part + refs[0][...] if last else part

    @pl.when(step > 0)
    def _():
        total[...] += part

    if last:

        @pl.when(step == pl.num_programs(0) - 1)
        def _():
            out_ref = refs[1]
            out_ref[...] = total[...].T[: out_ref.shape[0]]


def combine(back, main, late, feats, earlier=None, per_step=32):
    experts = back.shape[0]
    tokens = main.shape[0]
    last = earlier is not None
    steps = experts // per_step // 2
    base = steps if last else 0
    sums = pl.BlockSpec((tokens, 256), lambda i: (0, 0))
    out = pl.BlockSpec((feats, tokens), lambda i: (0, 0)) if last else sums
    return pl.pallas_call(
        functools.partial(combine_kernel, last),
        out_shape=jax.ShapeDtypeStruct((feats, tokens) if last else (tokens, 256), F32),
        grid=(steps,),
        in_specs=[
            pl.BlockSpec((per_step, PACK, 128), lambda i: (i + base, 0, 0)),
            pl.BlockSpec((tokens, per_step * 64), lambda i: (0, i + base)),
            pl.BlockSpec((tokens, per_step * 8), lambda i: (0, i + base)),
        ]
        + [sums] * last,
        out_specs=out,
        scratch_shapes=[pltpu.VMEM((tokens, 256), F32)] * last,
        compiler_params=params(("arbitrary",), 56 * 1024 * 1024),
        cost_estimate=pl.CostEstimate(
            flops=experts * 72 * 256 * tokens, bytes_accessed=12 * 10**6, transcendentals=0
        ),
    )(back, main, late, *([earlier] if last else []))


def finish_kernel(count, weights_a_ref, weights_b_ref, routed_ref, *refs):
    out_ref = refs[-1]
    half = out_ref.shape[1] // 2
    for i, weights_ref in enumerate((weights_a_ref, weights_b_ref)):
        units = jnp.concatenate([r[...] for r in refs[i * count : (i + 1) * count]], axis=0)
        cols = slice(i * half, (i + 1) * half)
        out = dot(weights_ref[...], units, ((1,), (0,)))
        out_ref[:, cols] = (out + routed_ref[:, cols]).astype(BF16)


def finish(weights_a, weights_b, routed, parts_a, parts_b):
    return pl.pallas_call(
        functools.partial(finish_kernel, len(parts_a)),
        out_shape=jax.ShapeDtypeStruct(routed.shape, BF16),
        in_specs=[whole()] * (3 + len(parts_a) + len(parts_b)),
        out_specs=whole(),
        compiler_params=params(vmem=20 * 1024 * 1024),
        cost_estimate=pl.CostEstimate(flops=10**9, bytes_accessed=7 * 10**6, transcendentals=0),
    )(weights_a, weights_b, routed, *parts_a, *parts_b)


def from_x(value, offset):
    pairs = [
        (y * SIDE + (x + offset) % SIDE, y * SIDE + x) for y in range(SIDE) for x in range(SIDE)
    ]
    return lax.ppermute(value, "tp", pairs)


def from_y(value, offset):
    pairs = [
        ((y + offset) % SIDE * SIDE + x, y * SIDE + x) for y in range(SIDE) for x in range(SIDE)
    ]
    return lax.ppermute(value, "tp", pairs)


OFFSETS = (0, 1, -1, 2)


def gather_halves(value, first, beside):
    half = value.shape[1] // 2
    a, b = value[:, :half], value[:, half:]
    line = [from_x(a, o) for o in OFFSETS[1:]] + [from_y(b, o) for o in OFFSETS[1:]]
    line, first = lax.optimization_barrier((line, first))
    a = jnp.concatenate([a] + line[:3], axis=0)
    b = jnp.concatenate([b] + line[3:], axis=0)
    near = (from_y(a, 1), from_y(a, -1), from_x(b, 1), from_x(b, -1))
    extra = beside(first)
    near, extra = lax.optimization_barrier((near, extra))
    a_next, a_prev, b_next, b_prev = near
    mid = a.shape[0] // 2
    far_a = [from_y(a_prev[:mid], -1), from_y(a_next[mid:], 1)]
    far_b = [from_x(b_prev[:mid], -1), from_x(b_next[mid:], 1)]
    return [a, a_next, a_prev] + far_a, [b, b_next, b_prev] + far_b, extra


def on_device(
    tokens,
    routes,
    route_weights,
    expert_owner,
    expert_gate_up,
    expert_down,
    shared_gate_up,
    shared_down,
):
    groups = lax.axis_size("dp")
    n_tensor = lax.axis_size("tp")
    experts = groups * n_tensor
    features = tokens.T
    features_all = lax.all_gather(features, "tp", axis=0, tiled=True)
    rank, weight, blocks = dispatch(
        routes.T, route_weights.T, expert_owner.reshape(1, -1), features
    )

    def exchange(blocks):
        return lax.all_to_all(blocks, ("dp", "tp"), split_axis=0, concat_axis=0, tiled=True)

    got = exchange(blocks).reshape(groups, n_tensor, PACK, 128)
    packed = expert(got, expert_gate_up[0], expert_down[0])

    rank, shared_down, _ = lax.optimization_barrier((rank, shared_down, packed))
    mine = lax.axis_index("tp")
    my_y, my_x = mine // SIDE, mine % SIDE
    ys = [(my_y + o) % SIDE * SIDE for o in OFFSETS]
    xs = [(my_x + o) % SIDE for o in OFFSETS]
    weights = shared_down.T.reshape(-1, n_tensor, shared_down.shape[0] // n_tensor)
    order_a = jnp.stack([y + x for y in ys for x in xs])
    order_b = jnp.stack([y + x for x in xs for y in ys])
    weights_a = jnp.take(weights, order_a, axis=1, mode="clip").reshape(weights.shape[0], -1)
    weights_b = jnp.take(weights, order_b, axis=1, mode="clip").reshape(weights.shape[0], -1)
    main, late = spread(rank, weight)
    back = exchange(packed.reshape(experts, PACK, 128))

    shared_gate_up, weights_a, weights_b, _ = lax.optimization_barrier(
        (shared_gate_up, weights_a, weights_b, late)
    )
    shared_w = shared_gate_up.reshape(features_all.shape[0], -1)
    proj = dot(shared_w, features_all, ((0,), (0,)))
    units = proj.shape[0] // 2
    shared_act = (jax.nn.silu(proj[:units]) * proj[units:]).astype(BF16)

    feats = features.shape[0]
    parts_a, parts_b, routed = gather_halves(
        shared_act,
        combine(back, main, late, feats),
        lambda earlier: combine(back, main, late, feats, earlier),
    )
    return finish(weights_a, weights_b, routed, parts_a, parts_b).T


def solution(mesh):
    return jax.shard_map(
        on_device,
        mesh=mesh,
        in_specs=(
            P("dp", "tp"),
            P("dp", None),
            P("dp", None),
            P(),
            P(("dp", "tp"), None, None),
            P(("dp", "tp"), None, None),
            P(None, None, "tp"),
            P(None, "tp"),
        ),
        out_specs=P("dp", "tp"),
        check_vma=False,
    )
```

```python
import functools

import jax
import jax.numpy as jnp
from jax import lax
from jax.experimental import pallas as pl
from jax.experimental.pallas import tpu as pltpu
from jax.sharding import PartitionSpec as P

F32 = jnp.float32
BF16 = jnp.bfloat16
SIDE = 4
ROW = 72
PACK = 120
VMEM = 40 * 1024 * 1024


def params(semantics=None, vmem=VMEM):
    return pltpu.CompilerParams(vmem_limit_bytes=vmem, dimension_semantics=semantics)


def whole(space=pltpu.VMEM):
    return pl.BlockSpec(memory_space=space)


def dot(a, b, dims):
    return lax.dot_general(a, b, (dims, ((), ())), preferred_element_type=F32)


def pack(low, high):
    lane = lax.broadcasted_iota(jnp.int32, (48, 128), 1)
    line = lax.broadcasted_iota(jnp.int32, (8, 128), 0)
    tail = high[48:64]
    moved = jnp.concatenate([pltpu.roll(tail, 96 - 32 * q, 1) for q in range(3)], axis=0)
    second = jnp.where(lane < 96, high[:48], moved)
    extra = jnp.where(line < 2, low[64:72], pltpu.roll(high[64:72], 2, 0))
    return jnp.concatenate([low[:64], second, extra], axis=0).astype(BF16)


def unpack_tail(second):
    lane = lax.broadcasted_iota(jnp.int32, (16, 128), 1)
    tail = jnp.zeros((16, 128), F32)
    for q in range(3):
        moved = pltpu.roll(second[16 * q : 16 * q + 16], 32 + 32 * q, 1)
        tail = jnp.where((lane >= 32 * q) & (lane < 32 * q + 32), moved, tail)
    return tail


def unpack(block):
    block = block.astype(F32)
    line = lax.broadcasted_iota(jnp.int32, (8, 128), 0)
    second, extra = block[64:112], block[112:120]
    low = jnp.concatenate([block[:64], jnp.where(line < 2, extra, 0.0)], axis=0)
    last = jnp.where(line < 2, pltpu.roll(extra, 6, 0), 0.0)
    high = jnp.concatenate([second, unpack_tail(second), last], axis=0)
    return jnp.concatenate([low, high[:, :96]], axis=1)


def dispatch_kernel(per_step, routes_ref, weights_ref, owner_ref, tokens_ref, rank_ref, weight_ref, out_ref):
    experts, tokens = rank_ref.shape
    feats = tokens_ref.shape[0]
    step = pl.program_id(0)

    @pl.when(step == 0)
    def _():
        owner = jnp.broadcast_to(owner_ref[...], (experts, experts)).astype(F32).T[:, :1]
        routes = routes_ref[...].astype(F32)
        hit = jnp.zeros((experts, tokens), F32)
        weight = jnp.zeros((experts, tokens), F32)
        for k in range(routes_ref.shape[0]):
            same = owner == routes[k : k + 1, :]
            hit = jnp.where(same, 1.0, hit)
            weight = jnp.where(same, weights_ref[k : k + 1, :], weight)
        weight_ref[...] = weight
        earlier = lax.broadcasted_iota(jnp.int32, (tokens, tokens), 0)
        later = lax.broadcasted_iota(jnp.int32, (tokens, tokens), 1)
        before = jnp.where(earlier < later, 1.0, 0.0).astype(BF16)
        rank = dot(hit.astype(BF16), before, ((1,), (0,)))
        rank_ref[...] = jnp.where(hit > 0.0, rank, -1.0)

    place = lax.broadcasted_iota(jnp.int32, (ROW, tokens), 0).astype(F32)
    rank = rank_ref[pl.ds(pl.multiple_of(step * per_step, per_step), per_step), :]
    pick = [jnp.where(place == rank[e : e + 1, :], 1.0, 0.0) for e in range(per_step)]
    pick = jnp.concatenate(pick, axis=0).astype(BF16)
    feat = jnp.concatenate([tokens_ref[...], jnp.zeros((256 - feats, tokens), BF16)], axis=0)
    res = dot(pick, feat, ((1,), (1,)))
    for e in range(per_step):
        rows = res[e * ROW : (e + 1) * ROW]
        out_ref[e] = pack(rows[:, :128], rows[:, 128:])


def dispatch(routes, weights, owner, tokens, per_step=16):
    experts, count = owner.shape[1], routes.shape[1]
    fixed = lambda a: pl.BlockSpec(a.shape, lambda i: (0, 0))
    table = jax.ShapeDtypeStruct((experts, count), F32)
    return pl.pallas_call(
        functools.partial(dispatch_kernel, per_step),
        out_shape=(table, table, jax.ShapeDtypeStruct((experts, PACK, 128), BF16)),
        grid=(experts // per_step,),
        in_specs=[fixed(routes), fixed(weights), fixed(owner), fixed(tokens)],
        out_specs=(
            fixed(table),
            fixed(table),
            pl.BlockSpec((per_step, PACK, 128), lambda i: (i, 0, 0)),
        ),
        compiler_params=params(("arbitrary",), 60 * 1024 * 1024),
        cost_estimate=pl.CostEstimate(
            flops=2 * experts * ROW * 256 * count, bytes_accessed=6 * 10**6, transcendentals=0
        ),
    )(routes, weights, owner, tokens)


def expert_kernel(tile, got_in, up_in, down_in, out_ref, got, up_w, down_w, x, act, held, sems):
    groups, n_tensor = out_ref.shape[:2]
    share = n_tensor // SIDE
    hidden = act.shape[1]
    wide = x.shape[1] // SIDE
    feats = wide // share
    tiles = hidden // tile

    def got_copy(k):
        return pltpu.make_async_copy(
            got_in.at[:, pl.ds(k * share, share)], got.at[k], sems.at[k]
        )

    def up_copy(n):
        cols = pl.ds(n * tile, tile)
        return pltpu.make_async_copy(up_in.at[:, cols], up_w.at[:, cols], sems.at[SIDE + n])

    def down_copy(y):
        cols = pl.ds(y * wide, wide)
        at = SIDE + 2 * tiles + y
        return pltpu.make_async_copy(down_in.at[:, cols], down_w.at[:, cols], sems.at[at])

    def out_copy(y):
        at = 2 * SIDE + 2 * tiles + y
        return pltpu.make_async_copy(
            held.at[y], out_ref.at[:, pl.ds(y * share, share)], sems.at[at]
        )

    for k in range(SIDE):
        got_copy(k).start()
    for n in range(tiles):
        up_copy(n).start()
        up_copy(tiles + n).start()
    for y in range(SIDE):
        down_copy(y).start()

    for k in range(SIDE):
        got_copy(k).wait()
        for d in range(0, groups, 2):
            rows = []
            for i in (d, d + 1):
                parts = [unpack(got[k, i, t]) for t in range(share)]
                rows.append(jnp.concatenate(parts, axis=1))
            x[d * ROW : (d + 2) * ROW, k * wide : (k + 1) * wide] = jnp.concatenate(
                rows, axis=0
            ).astype(BF16)

    for n in range(tiles):
        up_copy(n).wait()
        up_copy(tiles + n).wait()
        low = slice(n * tile, (n + 1) * tile)
        high = slice(hidden + n * tile, hidden + (n + 1) * tile)
        gate = dot(x[...], up_w[:, low], ((1,), (0,)))
        up = dot(x[...], up_w[:, high], ((1,), (0,)))
        act[:, low] = (gate / (1.0 + jnp.exp(-gate)) * up).astype(BF16)

    for y in range(SIDE):
        down_copy(y).wait()
        res = dot(act[...], down_w[:, y * wide : (y + 1) * wide], ((1,), (0,)))
        for t in range(share):
            low = res[:, t * feats : t * feats + 128]
            high = res[:, t * feats + 128 : (t + 1) * feats]
            blank = jnp.zeros((res.shape[0], 256 - feats), F32)
            high = jnp.concatenate([high, blank], axis=1)
            for d in range(groups):
                block = slice(d * ROW, (d + 1) * ROW)
                held[y, d, t] = pack(low[block], high[block])
        out_copy(y).start()
    for y in range(SIDE):
        out_copy(y).wait()


def expert(got, up_weights, down_weights, tile=256):
    groups, n_tensor = got.shape[:2]
    rows = groups * ROW
    width, both = up_weights.shape
    hidden = both // 2
    blocks = pltpu.VMEM((SIDE, groups, n_tensor // SIDE, PACK, 128), BF16)
    return pl.pallas_call(
        functools.partial(expert_kernel, tile),
        out_shape=jax.ShapeDtypeStruct(got.shape, BF16),
        in_specs=[whole(pl.ANY)] * 3,
        out_specs=whole(pl.ANY),
        scratch_shapes=[
            blocks,
            pltpu.VMEM((width, both), BF16),
            pltpu.VMEM((hidden, width), BF16),
            pltpu.VMEM((rows, width), BF16),
            pltpu.VMEM((rows, hidden), BF16),
            blocks,
            pltpu.SemaphoreType.DMA((3 * SIDE + both // tile,)),
        ],
        compiler_params=params(vmem=60 * 1024 * 1024),
        cost_estimate=pl.CostEstimate(
            flops=6 * rows * width * hidden, bytes_accessed=6 * width * hidden, transcendentals=0
        ),
    )(got, up_weights, down_weights)


def spread_kernel(rank_ref, weight_ref, main_ref, late_ref):
    experts, tokens = rank_ref.shape
    place = lax.broadcasted_iota(jnp.int32, (64, tokens), 0).astype(F32)
    line = lax.broadcasted_iota(jnp.int32, (8, tokens), 0)
    late = jnp.where(line < 4, jnp.where(line % 2 == 0, 64.0, 65.0), -2.0)
    extra = []
    for e in range(0, experts, 2):
        pair = []
        for i in (e, e + 1):
            rank = rank_ref[i : i + 1, :]
            weight = weight_ref[i : i + 1, :]
            pair.append(jnp.where(place == rank, weight, 0.0))
            extra.append(jnp.where(late == rank, weight, 0.0))
        main_ref[:, e * 64 : (e + 2) * 64] = jnp.concatenate(pair, axis=0).astype(BF16).T
    late_ref[...] = jnp.concatenate(extra, axis=0).astype(BF16).T


def spread(rank, weight, per_step=16):
    experts, tokens = rank.shape
    lines = pl.BlockSpec((per_step, tokens), lambda i: (i, 0))
    block = lambda rows: pl.BlockSpec((tokens, per_step * rows), lambda i: (0, i))
    return pl.pallas_call(
        spread_kernel,
        out_shape=(
            jax.ShapeDtypeStruct((tokens, experts * 64), BF16),
            jax.ShapeDtypeStruct((tokens, experts * 8), BF16),
        ),
        grid=(experts // per_step,),
        in_specs=[lines, lines],
        out_specs=(block(64), block(8)),
        compiler_params=params(("arbitrary",), 60 * 1024 * 1024),
        cost_estimate=pl.CostEstimate(
            flops=2 * experts * 64 * tokens, bytes_accessed=20 * 10**6, transcendentals=0
        ),
    )(rank, weight)


def combine_kernel(steps, back_ref, main_ref, late_ref, out_ref, total):
    step = pl.program_id(0)
    line = lax.broadcasted_iota(jnp.int32, (8, 128), 0)
    left, right, extra_l, extra_r = [], [], [], []
    for e in range(back_ref.shape[0]):
        left.append(back_ref[e, 0:64, :])
        second = back_ref[e, 64:112, :]
        tail = unpack_tail(second.astype(F32)).astype(BF16)
        right.append(jnp.concatenate([second, tail], axis=0))
        extra = back_ref[e, 112:120, :].astype(F32)
        extra_l.append(jnp.where(line < 2, extra, 0.0))
        extra_r.append(jnp.where((line >= 2) & (line < 4), extra, 0.0))
    rows = jnp.concatenate([jnp.concatenate(left, axis=0), jnp.concatenate(right, axis=0)], axis=1)
    late_rows = jnp.concatenate(
        [jnp.concatenate(extra_l, axis=0), jnp.concatenate(extra_r, axis=0)], axis=1
    ).astype(BF16)
    part = dot(main_ref[...], rows, ((1,), (0,))) + dot(late_ref[...], late_rows, ((1,), (0,)))

    @pl.when(step == 0)
    def _():
        total[...] = part

    @pl.when((step > 0) & (step < steps - 1))
    def _():
        total[...] += part

    @pl.when(step == steps - 1)
    def _():
        feats = out_ref.shape[0]
        out_ref[...] = (total[...] + part).T[:feats]


def combine(back, main, late, feats, per_step=32):
    experts = back.shape[0]
    tokens = main.shape[0]
    steps = experts // per_step
    return pl.pallas_call(
        functools.partial(combine_kernel, steps),
        out_shape=jax.ShapeDtypeStruct((feats, tokens), F32),
        grid=(steps,),
        in_specs=[
            pl.BlockSpec((per_step, PACK, 128), lambda i: (i, 0, 0)),
            pl.BlockSpec((tokens, per_step * 64), lambda i: (0, i)),
            pl.BlockSpec((tokens, per_step * 8), lambda i: (0, i)),
        ],
        out_specs=pl.BlockSpec((feats, tokens), lambda i: (0, 0)),
        scratch_shapes=[pltpu.VMEM((tokens, 256), F32)],
        compiler_params=params(("arbitrary",), 56 * 1024 * 1024),
        cost_estimate=pl.CostEstimate(
            flops=2 * experts * 72 * 256 * tokens, bytes_accessed=24 * 10**6, transcendentals=0
        ),
    )(back, main, late)


def finish_kernel(count, weights_a_ref, weights_b_ref, routed_ref, *refs):
    out_ref, routed, sem = refs[-3:]
    half = out_ref.shape[1] // 2
    copy = pltpu.make_async_copy(routed_ref, routed, sem)
    copy.start()
    for i, weights_ref in enumerate((weights_a_ref, weights_b_ref)):
        units = jnp.concatenate([r[...] for r in refs[i * count : (i + 1) * count]], axis=0)
        cols = slice(i * half, (i + 1) * half)
        out = dot(weights_ref[...], units, ((1,), (0,)))
        if i == 0:
            copy.wait()
        out_ref[:, cols] = (out + routed[:, cols]).astype(BF16)


def finish(weights_a, weights_b, routed, parts_a, parts_b):
    return pl.pallas_call(
        functools.partial(finish_kernel, len(parts_a)),
        out_shape=jax.ShapeDtypeStruct(routed.shape, BF16),
        in_specs=[whole(), whole(), whole(pl.ANY)] + [whole()] * (len(parts_a) + len(parts_b)),
        out_specs=whole(),
        scratch_shapes=[pltpu.VMEM(routed.shape, F32), pltpu.SemaphoreType.DMA],
        compiler_params=params(vmem=20 * 1024 * 1024),
        cost_estimate=pl.CostEstimate(flops=10**9, bytes_accessed=7 * 10**6, transcendentals=0),
    )(weights_a, weights_b, routed, *parts_a, *parts_b)


def from_x(value, offset):
    pairs = [
        (y * SIDE + (x + offset) % SIDE, y * SIDE + x) for y in range(SIDE) for x in range(SIDE)
    ]
    return lax.ppermute(value, "tp", pairs)


def from_y(value, offset):
    pairs = [
        ((y + offset) % SIDE * SIDE + x, y * SIDE + x) for y in range(SIDE) for x in range(SIDE)
    ]
    return lax.ppermute(value, "tp", pairs)


OFFSETS = (0, 1, -1, 2)


def gather_halves(value, beside):
    half = value.shape[1] // 2
    a, b = value[:, :half], value[:, half:]
    line = [from_x(a, o) for o in OFFSETS[1:]] + [from_y(b, o) for o in OFFSETS[1:]]
    line = lax.optimization_barrier(line)
    a = jnp.concatenate([a] + line[:3], axis=0)
    b = jnp.concatenate([b] + line[3:], axis=0)
    near = (from_y(a, 1), from_y(a, -1), from_x(b, 1), from_x(b, -1))
    near, extra = lax.optimization_barrier((near, beside(line[0])))
    a_next, a_prev, b_next, b_prev = near
    mid = a.shape[0] // 2
    far_a = [from_y(a_prev[:mid], -1), from_y(a_next[mid:], 1)]
    far_b = [from_x(b_prev[:mid], -1), from_x(b_next[mid:], 1)]
    return [a, a_next, a_prev] + far_a, [b, b_next, b_prev] + far_b, extra


def on_device(
    tokens,
    routes,
    route_weights,
    expert_owner,
    expert_gate_up,
    expert_down,
    shared_gate_up,
    shared_down,
):
    groups = lax.axis_size("dp")
    n_tensor = lax.axis_size("tp")
    experts = groups * n_tensor
    features = tokens.T
    features_all = lax.all_gather(features, "tp", axis=0, tiled=True)
    rank, weight, blocks = dispatch(
        routes.T, route_weights.T, expert_owner.reshape(1, -1), features
    )

    def exchange(blocks):
        return lax.all_to_all(blocks, ("dp", "tp"), split_axis=0, concat_axis=0, tiled=True)

    got = exchange(blocks).reshape(groups, n_tensor, PACK, 128)
    packed = expert(got, expert_gate_up[0], expert_down[0])

    rank, shared_down, _ = lax.optimization_barrier((rank, shared_down, packed))
    mine = lax.axis_index("tp")
    my_y, my_x = mine // SIDE, mine % SIDE
    ys = [(my_y + o) % SIDE * SIDE for o in OFFSETS]
    xs = [(my_x + o) % SIDE for o in OFFSETS]
    weights = shared_down.T.reshape(-1, n_tensor, shared_down.shape[0] // n_tensor)
    order_a = jnp.stack([y + x for y in ys for x in xs])
    order_b = jnp.stack([y + x for x in xs for y in ys])
    weights_a = jnp.take(weights, order_a, axis=1, mode="clip").reshape(weights.shape[0], -1)
    weights_b = jnp.take(weights, order_b, axis=1, mode="clip").reshape(weights.shape[0], -1)
    main, late = spread(rank, weight)
    back = exchange(packed.reshape(experts, PACK, 128))

    shared_gate_up, weights_a, weights_b, _ = lax.optimization_barrier(
        (shared_gate_up, weights_a, weights_b, late)
    )
    shared_w = shared_gate_up.reshape(features_all.shape[0], -1)
    proj = dot(shared_w, features_all, ((0,), (0,)))
    units = proj.shape[0] // 2
    shared_act = (jax.nn.silu(proj[:units]) * proj[units:]).astype(BF16)

    def beside(arrived):
        weights, _ = lax.optimization_barrier((late, arrived))
        return combine(back, main, weights, features.shape[0])

    parts_a, parts_b, routed = gather_halves(shared_act, beside)
    return finish(weights_a, weights_b, routed, parts_a, parts_b).T


def solution(mesh):
    return jax.shard_map(
        on_device,
        mesh=mesh,
        in_specs=(
            P("dp", "tp"),
            P("dp", None),
            P("dp", None),
            P(),
            P(("dp", "tp"), None, None),
            P(("dp", "tp"), None, None),
            P(None, None, "tp"),
            P(None, "tp"),
        ),
        out_specs=P("dp", "tp"),
        check_vma=False,
    )
```

```python
import functools

import jax
import jax.numpy as jnp
from jax import lax
from jax.experimental import pallas as pl
from jax.experimental.pallas import tpu as pltpu
from jax.sharding import PartitionSpec as P

F32 = jnp.float32
BF16 = jnp.bfloat16
SIDE = 4
ROW = 72
PACK = 120
VMEM = 40 * 1024 * 1024


def params(semantics=None, vmem=VMEM):
    return pltpu.CompilerParams(vmem_limit_bytes=vmem, dimension_semantics=semantics)


def whole(space=pltpu.VMEM):
    return pl.BlockSpec(memory_space=space)


def dot(a, b, dims):
    return lax.dot_general(a, b, (dims, ((), ())), preferred_element_type=F32)


def pack(low, high):
    lane = lax.broadcasted_iota(jnp.int32, (48, 128), 1)
    line = lax.broadcasted_iota(jnp.int32, (8, 128), 0)
    tail = high[48:64]
    moved = jnp.concatenate([pltpu.roll(tail, 96 - 32 * q, 1) for q in range(3)], axis=0)
    second = jnp.where(lane < 96, high[:48], moved)
    extra = jnp.where(line < 2, low[64:72], pltpu.roll(high[64:72], 2, 0))
    return jnp.concatenate([low[:64], second, extra], axis=0).astype(BF16)


def unpack_tail(second):
    lane = lax.broadcasted_iota(jnp.int32, (16, 128), 1)
    tail = jnp.zeros((16, 128), F32)
    for q in range(3):
        moved = pltpu.roll(second[16 * q : 16 * q + 16], 32 + 32 * q, 1)
        tail = jnp.where((lane >= 32 * q) & (lane < 32 * q + 32), moved, tail)
    return tail


def unpack(block):
    block = block.astype(F32)
    line = lax.broadcasted_iota(jnp.int32, (8, 128), 0)
    second, extra = block[64:112], block[112:120]
    low = jnp.concatenate([block[:64], jnp.where(line < 2, extra, 0.0)], axis=0)
    last = jnp.where(line < 2, pltpu.roll(extra, 6, 0), 0.0)
    high = jnp.concatenate([second, unpack_tail(second), last], axis=0)
    return jnp.concatenate([low, high[:, :96]], axis=1)


def dispatch_kernel(per_step, routes_ref, weights_ref, owner_ref, tokens_ref, rank_ref, weight_ref, out_ref):
    experts, tokens = rank_ref.shape
    feats = tokens_ref.shape[0]
    step = pl.program_id(0)

    @pl.when(step == 0)
    def _():
        owner = jnp.broadcast_to(owner_ref[...], (experts, experts)).astype(F32).T[:, :1]
        routes = routes_ref[...].astype(F32)
        hit = jnp.zeros((experts, tokens), F32)
        weight = jnp.zeros((experts, tokens), F32)
        for k in range(routes_ref.shape[0]):
            same = owner == routes[k : k + 1, :]
            hit = jnp.where(same, 1.0, hit)
            weight = jnp.where(same, weights_ref[k : k + 1, :], weight)
        weight_ref[...] = weight
        earlier = lax.broadcasted_iota(jnp.int32, (tokens, tokens), 0)
        later = lax.broadcasted_iota(jnp.int32, (tokens, tokens), 1)
        before = jnp.where(earlier < later, 1.0, 0.0).astype(BF16)
        rank = dot(hit.astype(BF16), before, ((1,), (0,)))
        rank_ref[...] = jnp.where(hit > 0.0, rank, -1.0)

    place = lax.broadcasted_iota(jnp.int32, (ROW, tokens), 0).astype(F32)
    rank = rank_ref[pl.ds(pl.multiple_of(step * per_step, per_step), per_step), :]
    pick = [jnp.where(place == rank[e : e + 1, :], 1.0, 0.0) for e in range(per_step)]
    pick = jnp.concatenate(pick, axis=0).astype(BF16)
    feat = jnp.concatenate([tokens_ref[...], jnp.zeros((256 - feats, tokens), BF16)], axis=0)
    res = dot(pick, feat, ((1,), (1,)))
    for e in range(per_step):
        rows = res[e * ROW : (e + 1) * ROW]
        out_ref[e] = pack(rows[:, :128], rows[:, 128:])


def dispatch(routes, weights, owner, tokens, per_step=16):
    experts, count = owner.shape[1], routes.shape[1]
    fixed = lambda a: pl.BlockSpec(a.shape, lambda i: (0, 0))
    table = jax.ShapeDtypeStruct((experts, count), F32)
    return pl.pallas_call(
        functools.partial(dispatch_kernel, per_step),
        out_shape=(table, table, jax.ShapeDtypeStruct((experts, PACK, 128), BF16)),
        grid=(experts // per_step,),
        in_specs=[fixed(routes), fixed(weights), fixed(owner), fixed(tokens)],
        out_specs=(
            fixed(table),
            fixed(table),
            pl.BlockSpec((per_step, PACK, 128), lambda i: (i, 0, 0)),
        ),
        compiler_params=params(("arbitrary",), 60 * 1024 * 1024),
        cost_estimate=pl.CostEstimate(
            flops=2 * experts * ROW * 256 * count, bytes_accessed=6 * 10**6, transcendentals=0
        ),
    )(routes, weights, owner, tokens)


def expert_kernel(tile, got_in, up_in, down_in, out_ref, got, up_w, down_w, x, act, held, sems):
    groups, n_tensor = out_ref.shape[:2]
    share = n_tensor // SIDE
    hidden = act.shape[1]
    wide = x.shape[1] // SIDE
    feats = wide // share
    tiles = hidden // tile

    def got_copy(k):
        return pltpu.make_async_copy(
            got_in.at[:, pl.ds(k * share, share)], got.at[k], sems.at[k]
        )

    def up_copy(n):
        cols = pl.ds(n * tile, tile)
        return pltpu.make_async_copy(up_in.at[:, cols], up_w.at[:, cols], sems.at[SIDE + n])

    def down_copy(y):
        cols = pl.ds(y * wide, wide)
        at = SIDE + 2 * tiles + y
        return pltpu.make_async_copy(down_in.at[:, cols], down_w.at[:, cols], sems.at[at])

    def out_copy(y):
        at = 2 * SIDE + 2 * tiles + y
        return pltpu.make_async_copy(
            held.at[y], out_ref.at[:, pl.ds(y * share, share)], sems.at[at]
        )

    for k in range(SIDE):
        got_copy(k).start()
    for n in range(tiles):
        up_copy(n).start()
        up_copy(tiles + n).start()
    for y in range(SIDE):
        down_copy(y).start()

    for k in range(SIDE):
        got_copy(k).wait()
        for d in range(0, groups, 2):
            rows = []
            for i in (d, d + 1):
                parts = [unpack(got[k, i, t]) for t in range(share)]
                rows.append(jnp.concatenate(parts, axis=1))
            x[d * ROW : (d + 2) * ROW, k * wide : (k + 1) * wide] = jnp.concatenate(
                rows, axis=0
            ).astype(BF16)

    for n in range(tiles):
        up_copy(n).wait()
        up_copy(tiles + n).wait()
        low = slice(n * tile, (n + 1) * tile)
        high = slice(hidden + n * tile, hidden + (n + 1) * tile)
        gate = dot(x[...], up_w[:, low], ((1,), (0,)))
        up = dot(x[...], up_w[:, high], ((1,), (0,)))
        act[:, low] = (gate / (1.0 + jnp.exp(-gate)) * up).astype(BF16)

    for y in range(SIDE):
        down_copy(y).wait()
        res = dot(act[...], down_w[:, y * wide : (y + 1) * wide], ((1,), (0,)))
        for t in range(share):
            low = res[:, t * feats : t * feats + 128]
            high = res[:, t * feats + 128 : (t + 1) * feats]
            blank = jnp.zeros((res.shape[0], 256 - feats), F32)
            high = jnp.concatenate([high, blank], axis=1)
            for d in range(groups):
                block = slice(d * ROW, (d + 1) * ROW)
                held[y, d, t] = pack(low[block], high[block])
        out_copy(y).start()
    for y in range(SIDE):
        out_copy(y).wait()


def expert(got, up_weights, down_weights, tile=256):
    groups, n_tensor = got.shape[:2]
    rows = groups * ROW
    width, both = up_weights.shape
    hidden = both // 2
    blocks = pltpu.VMEM((SIDE, groups, n_tensor // SIDE, PACK, 128), BF16)
    return pl.pallas_call(
        functools.partial(expert_kernel, tile),
        out_shape=jax.ShapeDtypeStruct(got.shape, BF16),
        in_specs=[whole(pl.ANY)] * 3,
        out_specs=whole(pl.ANY),
        scratch_shapes=[
            blocks,
            pltpu.VMEM((width, both), BF16),
            pltpu.VMEM((hidden, width), BF16),
            pltpu.VMEM((rows, width), BF16),
            pltpu.VMEM((rows, hidden), BF16),
            blocks,
            pltpu.SemaphoreType.DMA((3 * SIDE + both // tile,)),
        ],
        compiler_params=params(vmem=60 * 1024 * 1024),
        cost_estimate=pl.CostEstimate(
            flops=6 * rows * width * hidden, bytes_accessed=6 * width * hidden, transcendentals=0
        ),
    )(got, up_weights, down_weights)


def spread_kernel(rank_ref, weight_ref, main_ref, late_ref):
    experts, tokens = rank_ref.shape
    place = lax.broadcasted_iota(jnp.int32, (64, tokens), 0).astype(F32)
    line = lax.broadcasted_iota(jnp.int32, (8, tokens), 0)
    late = jnp.where(line < 4, jnp.where(line % 2 == 0, 64.0, 65.0), -2.0)
    extra = []
    for e in range(0, experts, 2):
        pair = []
        for i in (e, e + 1):
            rank = rank_ref[i : i + 1, :]
            weight = weight_ref[i : i + 1, :]
            pair.append(jnp.where(place == rank, weight, 0.0))
            extra.append(jnp.where(late == rank, weight, 0.0))
        main_ref[:, e * 64 : (e + 2) * 64] = jnp.concatenate(pair, axis=0).astype(BF16).T
    late_ref[...] = jnp.concatenate(extra, axis=0).astype(BF16).T


def spread(rank, weight, per_step=16):
    experts, tokens = rank.shape
    lines = pl.BlockSpec((per_step, tokens), lambda i: (i, 0))
    block = lambda rows: pl.BlockSpec((tokens, per_step * rows), lambda i: (0, i))
    return pl.pallas_call(
        spread_kernel,
        out_shape=(
            jax.ShapeDtypeStruct((tokens, experts * 64), BF16),
            jax.ShapeDtypeStruct((tokens, experts * 8), BF16),
        ),
        grid=(experts // per_step,),
        in_specs=[lines, lines],
        out_specs=(block(64), block(8)),
        compiler_params=params(("arbitrary",), 60 * 1024 * 1024),
        cost_estimate=pl.CostEstimate(
            flops=2 * experts * 64 * tokens, bytes_accessed=20 * 10**6, transcendentals=0
        ),
    )(rank, weight)


def combine_kernel(last, back_ref, main_ref, late_ref, *refs):
    step = pl.program_id(0)
    total = refs[-1]
    line = lax.broadcasted_iota(jnp.int32, (8, 128), 0)
    left, right, extra_l, extra_r = [], [], [], []
    for e in range(back_ref.shape[0]):
        left.append(back_ref[e, 0:64, :])
        second = back_ref[e, 64:112, :]
        tail = unpack_tail(second.astype(F32)).astype(BF16)
        right.append(jnp.concatenate([second, tail], axis=0))
        extra = back_ref[e, 112:120, :].astype(F32)
        extra_l.append(jnp.where(line < 2, extra, 0.0))
        extra_r.append(jnp.where((line >= 2) & (line < 4), extra, 0.0))
    rows = jnp.concatenate([jnp.concatenate(left, axis=0), jnp.concatenate(right, axis=0)], axis=1)
    late_rows = jnp.concatenate(
        [jnp.concatenate(extra_l, axis=0), jnp.concatenate(extra_r, axis=0)], axis=1
    ).astype(BF16)
    part = dot(main_ref[...], rows, ((1,), (0,))) + dot(late_ref[...], late_rows, ((1,), (0,)))

    @pl.when(step == 0)
    def _():
        total[...] = part + refs[0][...] if last else part

    @pl.when(step > 0)
    def _():
        total[...] += part

    if last:

        @pl.when(step == pl.num_programs(0) - 1)
        def _():
            out_ref = refs[1]
            out_ref[...] = total[...].T[: out_ref.shape[0]]


def combine(back, main, late, feats, earlier=None, per_step=32):
    experts = back.shape[0]
    tokens = main.shape[0]
    last = earlier is not None
    blocks = experts // per_step
    base = blocks // 4 if last else 0
    steps = blocks - base if last else blocks // 4
    sums = pl.BlockSpec((tokens, 256), lambda i: (0, 0))
    out = pl.BlockSpec((feats, tokens), lambda i: (0, 0)) if last else sums
    return pl.pallas_call(
        functools.partial(combine_kernel, last),
        out_shape=jax.ShapeDtypeStruct((feats, tokens) if last else (tokens, 256), F32),
        grid=(steps,),
        in_specs=[
            pl.BlockSpec((per_step, PACK, 128), lambda i: (i + base, 0, 0)),
            pl.BlockSpec((tokens, per_step * 64), lambda i: (0, i + base)),
            pl.BlockSpec((tokens, per_step * 8), lambda i: (0, i + base)),
        ]
        + [sums] * last,
        out_specs=out,
        scratch_shapes=[pltpu.VMEM((tokens, 256), F32)] * last,
        compiler_params=params(("arbitrary",), 56 * 1024 * 1024),
        cost_estimate=pl.CostEstimate(
            flops=2 * steps * per_step * 72 * 256 * tokens, bytes_accessed=steps * 6 * 10**6, transcendentals=0
        ),
    )(back, main, late, *([earlier] if last else []))


def finish_kernel(count, weights_a_ref, weights_b_ref, routed_ref, *refs):
    out_ref = refs[-1]
    half = out_ref.shape[1] // 2
    for i, weights_ref in enumerate((weights_a_ref, weights_b_ref)):
        units = jnp.concatenate([r[...] for r in refs[i * count : (i + 1) * count]], axis=0)
        cols = slice(i * half, (i + 1) * half)
        out = dot(weights_ref[...], units, ((1,), (0,)))
        out_ref[:, cols] = (out + routed_ref[:, cols]).astype(BF16)


def finish(weights_a, weights_b, routed, parts_a, parts_b):
    return pl.pallas_call(
        functools.partial(finish_kernel, len(parts_a)),
        out_shape=jax.ShapeDtypeStruct(routed.shape, BF16),
        in_specs=[whole()] * (3 + len(parts_a) + len(parts_b)),
        out_specs=whole(),
        compiler_params=params(vmem=20 * 1024 * 1024),
        cost_estimate=pl.CostEstimate(flops=10**9, bytes_accessed=7 * 10**6, transcendentals=0),
    )(weights_a, weights_b, routed, *parts_a, *parts_b)


def from_x(value, offset):
    pairs = [
        (y * SIDE + (x + offset) % SIDE, y * SIDE + x) for y in range(SIDE) for x in range(SIDE)
    ]
    return lax.ppermute(value, "tp", pairs)


def from_y(value, offset):
    pairs = [
        ((y + offset) % SIDE * SIDE + x, y * SIDE + x) for y in range(SIDE) for x in range(SIDE)
    ]
    return lax.ppermute(value, "tp", pairs)


OFFSETS = (0, 1, -1, 2)


def gather_halves(value, first, beside):
    half = value.shape[1] // 2
    a, b = value[:, :half], value[:, half:]
    line = [from_x(a, o) for o in OFFSETS[1:]] + [from_y(b, o) for o in OFFSETS[1:]]
    line, first = lax.optimization_barrier((line, first))
    a = jnp.concatenate([a] + line[:3], axis=0)
    b = jnp.concatenate([b] + line[3:], axis=0)
    near = (from_y(a, 1), from_y(a, -1), from_x(b, 1), from_x(b, -1))
    extra = beside(first)
    near, extra = lax.optimization_barrier((near, extra))
    a_next, a_prev, b_next, b_prev = near
    mid = a.shape[0] // 2
    far_a = [from_y(a_prev[:mid], -1), from_y(a_next[mid:], 1)]
    far_b = [from_x(b_prev[:mid], -1), from_x(b_next[mid:], 1)]
    return [a, a_next, a_prev] + far_a, [b, b_next, b_prev] + far_b, extra


def on_device(
    tokens,
    routes,
    route_weights,
    expert_owner,
    expert_gate_up,
    expert_down,
    shared_gate_up,
    shared_down,
):
    groups = lax.axis_size("dp")
    n_tensor = lax.axis_size("tp")
    experts = groups * n_tensor
    features = tokens.T
    features_all = lax.all_gather(features, "tp", axis=0, tiled=True)
    rank, weight, blocks = dispatch(
        routes.T, route_weights.T, expert_owner.reshape(1, -1), features
    )

    def exchange(blocks):
        return lax.all_to_all(blocks, ("dp", "tp"), split_axis=0, concat_axis=0, tiled=True)

    got = exchange(blocks).reshape(groups, n_tensor, PACK, 128)
    packed = expert(got, expert_gate_up[0], expert_down[0])

    rank, shared_down, _ = lax.optimization_barrier((rank, shared_down, packed))
    mine = lax.axis_index("tp")
    my_y, my_x = mine // SIDE, mine % SIDE
    ys = [(my_y + o) % SIDE * SIDE for o in OFFSETS]
    xs = [(my_x + o) % SIDE for o in OFFSETS]
    weights = shared_down.T.reshape(-1, n_tensor, shared_down.shape[0] // n_tensor)
    order_a = jnp.stack([y + x for y in ys for x in xs])
    order_b = jnp.stack([y + x for x in xs for y in ys])
    weights_a = jnp.take(weights, order_a, axis=1, mode="clip").reshape(weights.shape[0], -1)
    weights_b = jnp.take(weights, order_b, axis=1, mode="clip").reshape(weights.shape[0], -1)
    main, late = spread(rank, weight)
    back = exchange(packed.reshape(experts, PACK, 128))

    shared_gate_up, weights_a, weights_b, _ = lax.optimization_barrier(
        (shared_gate_up, weights_a, weights_b, late)
    )
    shared_w = shared_gate_up.reshape(features_all.shape[0], -1)
    proj = dot(shared_w, features_all, ((0,), (0,)))
    units = proj.shape[0] // 2
    shared_act = (jax.nn.silu(proj[:units]) * proj[units:]).astype(BF16)

    feats = features.shape[0]
    parts_a, parts_b, routed = gather_halves(
        shared_act,
        combine(back, main, late, feats),
        lambda earlier: combine(back, main, late, feats, earlier),
    )
    return finish(weights_a, weights_b, routed, parts_a, parts_b).T


def solution(mesh):
    return jax.shard_map(
        on_device,
        mesh=mesh,
        in_specs=(
            P("dp", "tp"),
            P("dp", None),
            P("dp", None),
            P(),
            P(("dp", "tp"), None, None),
            P(("dp", "tp"), None, None),
            P(None, None, "tp"),
            P(None, "tp"),
        ),
        out_specs=P("dp", "tp"),
        check_vma=False,
    )
```
